32 devices in a mesh: group: 2 (over y), passage: 4 (over z), span: 4 (over x, core).
Axes of the slice: x: 2, y: 2, z: 4, core: 2. Of those that a mesh axis runs over, the one named last changes fastest.
Arguments:
- flow_state: float32 [64, 1024, 4096], P('group', 'span', 'passage'), parts along dimension 0, may hold values from -6 to 6
- swirl_speed: float32 [2048], P(('group', 'span')), parts along dimension 0, may hold values from -0.8 to 0.8
- diffusivity: float32 [2048, 4096], P(('group', 'span'), 'passage'), parts along dimension 0, may hold values from 0.02 to 0.2
- plane_index: int32 [16], P('group'), parts along dimension 0, may hold values from 0 to 31, as said below
- radial_modes: float32 [64, 1024], P(None, 'span'), may hold values from -0.1875 to 0.1875
- mode_order: int32 [64], replicated, may hold values from 0 to 63, each once
Outputs:
- next_state: float32 [64, 1024, 4096], P('group', 'span', 'passage'), parts along dimension 0
- amplitudes: float32 [16, 64, 256], P('group'), parts along dimension 0
The draws below stay inside these ranges and needn't reach their ends.
There are 2 independent parts, one for each index of `group`. The reference program is written for one: setup_inputs(seed, part) draws one part's arguments, and reference() takes and returns one part's arrays. A program takes and returns all parts, laid end to end along the dimension named above; an argument that names none is the same for every part. Nothing has to cross between parts.
Inputs may be any that keep to these rules, and one draw needn't show every extreme that they name: `plane_index`: distinct stations, one of them station 32 - 1. `mode_order`: each number once.
All inputs are finite; a program needn't handle non-finite values.
Results may differ from the reference program's by a relative error of at most 0.000071.
Values sent between devices are 32-bit elements; how exact they have to be, the bound alone decides.
A program may use at most 128 MiB of HBM per device.

```python
import math
import jax
import jax.numpy as jnp
from jax import lax

NZ = 32
NR = 1024
NTH = 4096
PL = 8
BLADES = 16
K = 128
M = 64


def draw_plane_index(key, part):
    first_key = jax.random.fold_in(key, 11)
    second_key = jax.random.fold_in(key, 23)
    others = jax.random.permutation(first_key, NZ - 1)[:PL - 1].astype(jnp.int32)
    stations = jnp.concatenate([others, jnp.full((1,), NZ - 1, dtype=jnp.int32)])
    return jax.random.permutation(second_key, stations).astype(jnp.int32)


def shard_levels(stream_key, shape, split, least, largest):
    def one(dim, blocks):
        draws = jax.random.uniform(jax.random.fold_in(jax.random.fold_in(stream_key, 6), dim), (blocks,), jnp.float32, least / len(split), largest / len(split))
        return jnp.repeat(jnp.exp(draws), shape[dim] // blocks).reshape((-1,) + (1,) * (len(shape) - dim - 1))

    factor_of = one(*split[0])
    for cut in split[1:]:
        factor_of = factor_of * one(*cut)
    return factor_of


def gaussian(own_key, shape, spread, reach, cuts=(), held_as=jnp.bfloat16):
    values = spread * jax.random.normal(own_key, shape, jnp.float32)
    if cuts:
        values = values * shard_levels(own_key, shape, cuts, -0.22, 0.18)
    return jnp.clip(values, -reach, reach).astype(held_as)


def setup_inputs(seed: int = 0, part: int = 0) -> dict:
    splits = jax.random.split(jax.random.key(seed), 7)
    part_splits = jax.random.split(jax.random.fold_in(splits[6], part), 7)
    flow_state = gaussian(part_splits[0], (NZ, NR, NTH), 1.0, 6.0, ((1, 4), (2, 4)), jnp.float32)
    swirl_speed = jnp.clip(jax.random.uniform(part_splits[1], (NR,), jnp.float32, -0.8, 0.8) * shard_levels(part_splits[1], (NR,), ((0, 4),), -0.4, 0.0), -0.8, 0.8)
    diffusivity = jnp.clip(jnp.exp(math.log(0.2) - 2.3025851 * jax.random.uniform(part_splits[2], (NR, NTH), jnp.float32) ** shard_levels(part_splits[2], (NR, NTH), ((0, 4), (1, 4)), -0.2, 0.2)), 0.02, 0.2)
    plane_index = draw_plane_index(jax.random.fold_in(jax.random.fold_in(splits[6], part), 71), part)
    radial_modes = gaussian(splits[4], (M, NR), NR ** -0.5, 0.1875, ((1, 4),), jnp.float32)
    mode_order = jax.random.permutation(splits[5], M).astype(jnp.int32)
    return dict(flow_state=flow_state, swirl_speed=swirl_speed, diffusivity=diffusivity, plane_index=plane_index, radial_modes=radial_modes, mode_order=mode_order)


def spectra_basis(offset, extent, period, harmonics, blades):
    azimuth = (offset + jnp.arange(extent, dtype=jnp.int32))[:, None]
    harmonic = (jnp.arange(harmonics, dtype=jnp.int32) * blades)[None, :]
    phases = azimuth * harmonic % period
    angles = phases.astype(jnp.float32) * (2.0 * math.pi / period)
    return jnp.concatenate([jnp.cos(angles), -jnp.sin(angles)], axis=1) * (1.0 / math.sqrt(period))

def reference(flow_state, swirl_speed, diffusivity, plane_index, radial_modes, mode_order):
    east_cell = jnp.roll(flow_state, -1, axis=2)
    west_cell = jnp.roll(flow_state, 1, axis=2)
    padded = jnp.pad(flow_state, ((0, 0), (1, 1), (0, 0)))
    outer_cell = padded[:, 2:, :]
    inner_cell = padded[:, :-2, :]
    next_state = flow_state - 0.5 * swirl_speed[None, :, None] * (east_cell - west_cell) + diffusivity[None] * (east_cell + west_cell + outer_cell + inner_cell - 4.0 * flow_state)
    chosen = jnp.take(next_state, plane_index, axis=0)
    basis = spectra_basis(0, NTH, NTH, K, BLADES)
    spectra = jnp.einsum('prt,tc->prc', chosen, basis, precision=lax.Precision.HIGHEST)
    picked = jnp.take(radial_modes, mode_order, axis=0)
    amplitudes = jnp.einsum('mr,prc->pmc', picked, spectra, precision=lax.Precision.HIGHEST)
    return (next_state, amplitudes)
```

```python
import functools
import math

import jax
import jax.numpy as jnp
import numpy as np
from jax import lax
from jax.experimental import pallas as pl
from jax.experimental.pallas import tpu as pltpu
from jax.sharding import PartitionSpec as P

NTH = 4096
BLADES = 16
K = 128
PERIOD = NTH // BLADES
LANES = 128
MIB = 1024 * 1024
MESH = pl.DeviceIdType.MESH


def dft_basis():
    t = np.arange(PERIOD)[:, None]
    k = np.arange(K)[None, :]
    angles = (t * k % PERIOD) * (2.0 * math.pi / PERIOD)
    both = np.concatenate([np.cos(angles), -np.sin(angles)], axis=1)
    return (both / math.sqrt(NTH)).astype(np.float32)


def halo_kernel(
    passages, spans, chunks, flow, rows_out, cols_out,
    left, right, low, high, rows_send, cols_send, load_sem, send_sem, recv_sem,
):
    stations, rows, cols = flow.shape
    passage = lax.axis_index("passage")
    span = lax.axis_index("span")
    groups = LANES // stations
    per = rows // groups
    step = stations // chunks

    def loads(c):
        part = pl.ds(c * step, step)
        return [
            pltpu.make_async_copy(
                flow.at[part, :, pl.ds(0, LANES)], left.at[part], load_sem.at[2 + 2 * c]),
            pltpu.make_async_copy(
                flow.at[part, :, pl.ds(cols - LANES, LANES)], right.at[part],
                load_sem.at[3 + 2 * c]),
        ]

    row_loads = [
        pltpu.make_async_copy(flow.at[:, pl.ds(0, 8), :], low, load_sem.at[0]),
        pltpu.make_async_copy(flow.at[:, pl.ds(rows - 8, 8), :], high, load_sem.at[1]),
    ]
    for copy in row_loads:
        copy.start()
    for c in range(chunks):
        for copy in loads(c):
            copy.start()

    west = lax.rem(passage + passages - 1, passages)
    east = lax.rem(passage + 1, passages)
    outer = jnp.minimum(span + 1, spans - 1)
    inner = jnp.maximum(span - 1, 0)
    barrier = pltpu.get_barrier_semaphore()
    for side in (west, east):
        pl.semaphore_signal(barrier, inc=1, device_id={"passage": side}, device_id_type=MESH)
    for side in (1, spans - 1):
        pl.semaphore_signal(
            barrier, inc=1, device_id={"span": lax.rem(span + side, spans)}, device_id_type=MESH)
    pl.semaphore_wait(barrier, 4)

    to_inner = pltpu.make_async_remote_copy(
        src_ref=rows_send.at[0], dst_ref=rows_out.at[1], send_sem=send_sem.at[0],
        recv_sem=recv_sem.at[0], device_id={"span": inner}, device_id_type=MESH)
    to_outer = pltpu.make_async_remote_copy(
        src_ref=rows_send.at[1], dst_ref=rows_out.at[0], send_sem=send_sem.at[1],
        recv_sem=recv_sem.at[1], device_id={"span": outer}, device_id_type=MESH)
    to_west = pltpu.make_async_remote_copy(
        src_ref=cols_send.at[0], dst_ref=cols_out.at[1], send_sem=send_sem.at[2],
        recv_sem=recv_sem.at[2], device_id={"passage": west}, device_id_type=MESH)
    to_east = pltpu.make_async_remote_copy(
        src_ref=cols_send.at[1], dst_ref=cols_out.at[0], send_sem=send_sem.at[3],
        recv_sem=recv_sem.at[3], device_id={"passage": east}, device_id_type=MESH)

    for copy in row_loads:
        copy.wait()
    rows_send[0] = low[:, 0, :]
    rows_send[1] = high[:, 7, :]

    @pl.when(span > 0)
    def _():
        to_inner.start()

    @pl.when(span < spans - 1)
    def _():
        to_outer.start()

    @pl.when(span == 0)
    def _():
        rows_out[0] = jnp.zeros((stations, cols), jnp.float32)

    @pl.when(span == spans - 1)
    def _():
        rows_out[1] = jnp.zeros((stations, cols), jnp.float32)

    lane = lax.broadcasted_iota(jnp.int32, (per, LANES), 1)

    def pack(z, carry):
        a, b = carry
        for g in range(groups):
            spot = g * stations + z
            part = pl.ds(g * per, per)
            a = jnp.where(lane == spot, pltpu.roll(left[z, part, :], spot, 1), a)
            b = jnp.where(lane == spot, pltpu.roll(right[z, part, :], spot + 1, 1), b)
        return a, b

    zero = jnp.zeros((per, LANES), jnp.float32)
    carry = (zero, zero)
    for c in range(chunks):
        for copy in loads(c):
            copy.wait()
        carry = lax.fori_loop(c * step, (c + 1) * step, pack, carry)
    cols_send[0], cols_send[1] = carry
    to_west.start()
    to_east.start()
    to_west.wait()
    to_east.wait()

    @pl.when(span > 0)
    def _():
        to_inner.wait_send()
        to_outer.wait_recv()

    @pl.when(span < spans - 1)
    def _():
        to_outer.wait_send()
        to_inner.wait_recv()


def halo(flow, passages, spans):
    stations, rows, cols = flow.shape
    groups = LANES // stations
    chunks = 4
    f32 = jnp.float32
    vmem = pl.BlockSpec(memory_space=pltpu.VMEM)
    return pl.pallas_call(
        functools.partial(halo_kernel, passages, spans, chunks),
        out_shape=(
            jax.ShapeDtypeStruct((2, stations, cols), f32),
            jax.ShapeDtypeStruct((2, rows // groups, LANES), f32),
        ),
        in_specs=[pl.BlockSpec(memory_space=pl.ANY)],
        out_specs=(vmem, vmem),
        scratch_shapes=[
            pltpu.VMEM((stations, rows, LANES), f32),
            pltpu.VMEM((stations, rows, LANES), f32),
            pltpu.VMEM((stations, 8, cols), f32),
            pltpu.VMEM((stations, 8, cols), f32),
            pltpu.VMEM((2, stations, cols), f32),
            pltpu.VMEM((2, rows // groups, LANES), f32),
            pltpu.SemaphoreType.DMA((2 + 2 * chunks,)),
            pltpu.SemaphoreType.DMA((4,)),
            pltpu.SemaphoreType.DMA((4,)),
        ],
        compiler_params=pltpu.CompilerParams(
            collective_id=0, has_side_effects=True, vmem_limit_bytes=24 * MIB),
        name="halo",
    )(flow)


def stencil_kernel(
    planes, plane_index, mode_order, flow, rows_in, cols_in, swirl, diff, modes, basis,
    out, amp, coef_e, coef_w, coef_c, picked, fold,
):
    _, rows, cols = flow.shape
    stations = rows_in.shape[1]
    per = cols_in.shape[1]
    z = pl.program_id(0)

    @pl.when(z == 0)
    def _():
        d = diff[...]
        half = 0.5 * jnp.broadcast_to(swirl[...], (LANES, rows)).T
        half = jnp.concatenate([half] * (cols // LANES), axis=1)
        coef_e[...] = d - half
        coef_w[...] = d + half
        coef_c[...] = 1.0 - 4.0 * d
        for j in range(modes.shape[0]):
            picked[pl.ds(j, 1), :] = modes[pl.ds(mode_order[j], 1), :]

    lane = lax.broadcasted_iota(jnp.int32, (8, LANES), 1)
    sub = lax.broadcasted_iota(jnp.int32, (8, cols), 0)
    last = cols - LANES
    for r in range(0, rows, 8):
        part = slice(r, r + 8)
        center = flow[0, part, :]
        if r == 0:
            inner = jnp.where(sub == 0, rows_in[0, pl.ds(z, 1), :], pltpu.roll(center, 1, 0))
        else:
            inner = flow[0, r - 1:r + 7, :]
        if r == rows - 8:
            outer = jnp.where(sub == 7, rows_in[1, pl.ds(z, 1), :], pltpu.roll(center, 7, 0))
        else:
            outer = flow[0, r + 1:r + 9, :]
        spot = (r // per) * stations + z
        packed = slice(r % per, r % per + 8)
        west_edge = pltpu.roll(cols_in[0, packed, :], LANES - spot, 1)
        east_edge = pltpu.roll(cols_in[1, packed, :], LANES - 1 - spot, 1)
        east = pltpu.roll(center, cols - 1, 1)
        west = pltpu.roll(center, 1, 1)
        east = jnp.concatenate(
            [east[:, :last], jnp.where(lane == LANES - 1, east_edge, east[:, last:])], axis=1)
        west = jnp.concatenate(
            [jnp.where(lane == 0, west_edge, west[:, :LANES]), west[:, LANES:]], axis=1)
        value = (
            coef_c[part, :] * center + coef_e[part, :] * east + coef_w[part, :] * west
            + diff[part, :] * (outer + inner)
        )
        out[0, part, :] = value
        total = value[:, :PERIOD]
        for m in range(PERIOD, cols, PERIOD):
            total = total + value[:, m:m + PERIOD]
        fold[part, :] = total

    for p in range(planes):
        @pl.when(plane_index[p] == z)
        def _():
            shape = jnp.dot(
                picked[...], fold[...], precision=lax.Precision.HIGHEST,
                preferred_element_type=jnp.float32)
            lines = jnp.dot(
                shape, basis[...], precision=lax.Precision.HIGHEST,
                preferred_element_type=jnp.float32)
            tiles = lines.shape[0] // 8
            for h in range(2):
                amp[pl.ds((2 * p + h) * tiles, tiles)] = (
                    lines[:, h * LANES:(h + 1) * LANES].reshape(tiles, 8, LANES))


def stencil(flow, rows_in, cols_in, swirl, diff, plane_index, modes, mode_order):
    stations, rows, cols = flow.shape
    planes = plane_index.shape[0]
    m = modes.shape[0]
    f32 = jnp.float32
    smem = pl.BlockSpec(memory_space=pltpu.SMEM)
    plane = pl.BlockSpec((1, rows, cols), lambda z: (z, 0, 0))

    def whole(shape):
        return pl.BlockSpec(shape, lambda z: (0,) * len(shape))

    tiles = planes * m * 2 * K // (8 * LANES)
    return pl.pallas_call(
        functools.partial(stencil_kernel, planes),
        out_shape=(
            jax.ShapeDtypeStruct(flow.shape, f32),
            jax.ShapeDtypeStruct((tiles, 8, LANES), f32),
        ),
        grid=(stations,),
        in_specs=[
            smem, smem, plane, whole(rows_in.shape), whole(cols_in.shape), whole((1, rows)),
            whole(diff.shape), whole(modes.shape), whole((PERIOD, 2 * K)),
        ],
        out_specs=(plane, whole((tiles, 8, LANES))),
        scratch_shapes=[
            pltpu.VMEM((rows, cols), f32),
            pltpu.VMEM((rows, cols), f32),
            pltpu.VMEM((rows, cols), f32),
            pltpu.VMEM((m, rows), f32),
            pltpu.VMEM((rows, PERIOD), f32),
        ],
        compiler_params=pltpu.CompilerParams(vmem_limit_bytes=32 * MIB),
        name="stencil",
    )(plane_index, mode_order, flow, rows_in, cols_in, swirl.reshape(1, rows), diff, modes,
      jnp.asarray(dft_basis()))


def sum_kernel(sizes, amp, out, acc, full, *rest):
    recvs, (send_sem, recv_sem, send_sem2, recv_sem2) = rest[:3], rest[3:]
    cores, xs, zs = sizes
    span = lax.axis_index("span")
    core, x, z = lax.rem(span, cores), span // cores, lax.axis_index("passage")
    mine = (core, x, z)

    def peer(s, k):
        if s == 0:
            return {"span": x * cores + k}
        if s == 1:
            return {"span": k * cores + core}
        return {"passage": k}

    def others(s):
        return [(d, lax.rem(mine[s] + d, sizes[s])) for d in range(1, sizes[s])]

    barrier = pltpu.get_barrier_semaphore()
    for s in range(3):
        for _, k in others(s):
            pl.semaphore_signal(barrier, inc=1, device_id=peer(s, k), device_id_type=MESH)
    pl.semaphore_wait(barrier, sum(sizes) - 3)

    size = amp.shape[0]
    base = 0
    bases, widths = [], []
    index = 0
    firsts = []
    for s in range(3):
        width = size // sizes[s]
        source = amp if s == 0 else acc
        firsts.append(index)
        copies = []
        for d, k in others(s):
            copy = pltpu.make_async_remote_copy(
                src_ref=source.at[pl.ds(base + k * width, width)], dst_ref=recvs[s].at[d - 1],
                send_sem=send_sem.at[index], recv_sem=recv_sem.at[index],
                device_id=peer(s, k), device_id_type=MESH)
            copy.start()
            copies.append(copy)
            index += 1
        base = base + mine[s] * width
        size = width
        bases.append(base)
        widths.append(width)
        for copy in copies:
            copy.wait()
        part = pl.ds(base, width)
        total = source[part]
        for d in range(1, sizes[s]):
            total = total + recvs[s][d - 1]
        if s < 2:
            acc[part] = total
        else:
            full[part] = total

    for s in (2, 1, 0):
        part = pl.ds(bases[s], widths[s])
        copies = []
        for d, k in others(s):
            at = firsts[s] + d - 1
            copy = pltpu.make_async_remote_copy(
                src_ref=full.at[part], dst_ref=full.at[part],
                send_sem=send_sem2.at[at], recv_sem=recv_sem2.at[at],
                device_id=peer(s, k), device_id_type=MESH)
            copy.start()
            copies.append(copy)
        for copy in copies:
            copy.wait()

    planes, m, _ = out.shape
    tiles = m // 8
    for p in range(planes):
        for h in range(2):
            out[p, :, h * LANES:(h + 1) * LANES] = (
                full[pl.ds((2 * p + h) * tiles, tiles)].reshape(m, LANES))


def amplitude_sum(amp, planes, m, sizes):
    f32 = jnp.float32
    tiles = amp.shape[0]
    widths = [tiles // math.prod(sizes[:s + 1]) for s in range(3)]
    total = sum(sizes) - 3
    vmem = pl.BlockSpec(memory_space=pltpu.VMEM)
    return pl.pallas_call(
        functools.partial(sum_kernel, sizes),
        out_shape=jax.ShapeDtypeStruct((planes, m, 2 * K), f32),
        in_specs=[vmem],
        out_specs=vmem,
        scratch_shapes=[
            pltpu.VMEM((tiles, 8, LANES), f32),
            pltpu.VMEM((tiles, 8, LANES), f32),
            *[pltpu.VMEM((max(n - 1, 1), w, 8, LANES), f32) for n, w in zip(sizes, widths)],
            *[pltpu.SemaphoreType.DMA((total,)) for _ in range(4)],
        ],
        compiler_params=pltpu.CompilerParams(
            collective_id=1, has_side_effects=True, vmem_limit_bytes=16 * MIB),
        name="amplitude_sum",
    )(amp)


def body(passages, spans, flow_state, swirl_speed, diffusivity, plane_index, radial_modes, mode_order):
    rows_in, cols_in = halo(flow_state, passages, spans)
    next_state, partial_value = stencil(
        flow_state, rows_in, cols_in, swirl_speed, diffusivity, plane_index, radial_modes, mode_order)
    sizes = (2, spans // 2, passages)
    amplitudes = amplitude_sum(partial_value, plane_index.shape[0], mode_order.shape[0], sizes)
    return (next_state, amplitudes)


def solution(mesh):
    return jax.shard_map(
        functools.partial(body, mesh.shape["passage"], mesh.shape["span"]),
        mesh=mesh,
        in_specs=(
            P("group", "span", "passage"),
            P(("group", "span")),
            P(("group", "span"), "passage"),
            P("group"),
            P(None, "span"),
            P(),
        ),
        out_specs=(P("group", "span", "passage"), P("group", None, None)),
        check_vma=False,
    )
```

```python
import functools
import math

import jax
import jax.numpy as jnp
import numpy as np
from jax import lax
from jax.experimental import pallas as pl
from jax.experimental.pallas import tpu as pltpu
from jax.sharding import PartitionSpec as P

NTH = 4096
BLADES = 16
K = 128
PERIOD = NTH // BLADES
LANES = 128
MIB = 1024 * 1024
MESH = pl.DeviceIdType.MESH


def dft_basis():
    t = np.arange(PERIOD)[:, None]
    k = np.arange(K)[None, :]
    angles = (t * k % PERIOD) * (2.0 * math.pi / PERIOD)
    both = np.concatenate([np.cos(angles), -np.sin(angles)], axis=1)
    return (both / math.sqrt(NTH)).astype(np.float32)


def halo_kernel(
    passages, spans, chunks, flow, rows_out, cols_out,
    left, right, low, high, rows_send, cols_send, load_sem, send_sem, recv_sem,
):
    stations, rows, cols = flow.shape
    passage = lax.axis_index("passage")
    span = lax.axis_index("span")
    groups = LANES // stations
    per = rows // groups
    step = stations // chunks

    def loads(c):
        part = pl.ds(c * step, step)
        return [
            pltpu.make_async_copy(
                flow.at[part, :, pl.ds(0, LANES)], left.at[part], load_sem.at[2 + 2 * c]),
            pltpu.make_async_copy(
                flow.at[part, :, pl.ds(cols - LANES, LANES)], right.at[part],
                load_sem.at[3 + 2 * c]),
        ]

    row_loads = [
        pltpu.make_async_copy(flow.at[:, pl.ds(0, 8), :], low, load_sem.at[0]),
        pltpu.make_async_copy(flow.at[:, pl.ds(rows - 8, 8), :], high, load_sem.at[1]),
    ]
    for copy in row_loads:
        copy.start()
    for c in range(chunks):
        for copy in loads(c):
            copy.start()

    west = lax.rem(passage + passages - 1, passages)
    east = lax.rem(passage + 1, passages)
    outer = jnp.minimum(span + 1, spans - 1)
    inner = jnp.maximum(span - 1, 0)
    barrier = pltpu.get_barrier_semaphore()
    for side in (west, east):
        pl.semaphore_signal(barrier, inc=1, device_id={"passage": side}, device_id_type=MESH)
    for side in (1, spans - 1):
        pl.semaphore_signal(
            barrier, inc=1, device_id={"span": lax.rem(span + side, spans)}, device_id_type=MESH)
    pl.semaphore_wait(barrier, 4)

    to_inner = pltpu.make_async_remote_copy(
        src_ref=rows_send.at[0], dst_ref=rows_out.at[1], send_sem=send_sem.at[0],
        recv_sem=recv_sem.at[0], device_id={"span": inner}, device_id_type=MESH)
    to_outer = pltpu.make_async_remote_copy(
        src_ref=rows_send.at[1], dst_ref=rows_out.at[0], send_sem=send_sem.at[1],
        recv_sem=recv_sem.at[1], device_id={"span": outer}, device_id_type=MESH)
    to_west = pltpu.make_async_remote_copy(
        src_ref=cols_send.at[0], dst_ref=cols_out.at[1], send_sem=send_sem.at[2],
        recv_sem=recv_sem.at[2], device_id={"passage": west}, device_id_type=MESH)
    to_east = pltpu.make_async_remote_copy(
        src_ref=cols_send.at[1], dst_ref=cols_out.at[0], send_sem=send_sem.at[3],
        recv_sem=recv_sem.at[3], device_id={"passage": east}, device_id_type=MESH)

    for copy in row_loads:
        copy.wait()
    rows_send[0] = low[:, 0, :]
    rows_send[1] = high[:, 7, :]

    @pl.when(span > 0)
    def _():
        to_inner.start()

    @pl.when(span < spans - 1)
    def _():
        to_outer.start()

    @pl.when(span == 0)
    def _():
        rows_out[0] = jnp.zeros((stations, cols), jnp.float32)

    @pl.when(span == spans - 1)
    def _():
        rows_out[1] = jnp.zeros((stations, cols), jnp.float32)

    lane = lax.broadcasted_iota(jnp.int32, (per, LANES), 1)

    def pack(z, carry):
        a, b = carry
        for g in range(groups):
            spot = g * stations + z
            part = pl.ds(g * per, per)
            a = jnp.where(lane == spot, pltpu.roll(left[z, part, :], spot, 1), a)
            b = jnp.where(lane == spot, pltpu.roll(right[z, part, :], spot + 1, 1), b)
        return a, b

    zero = jnp.zeros((per, LANES), jnp.float32)
    carry = (zero, zero)
    for c in range(chunks):
        for copy in loads(c):
            copy.wait()
        carry = lax.fori_loop(c * step, (c + 1) * step, pack, carry)
    cols_send[0], cols_send[1] = carry
    to_west.start()
    to_east.start()
    to_west.wait()
    to_east.wait()

    @pl.when(span > 0)
    def _():
        to_inner.wait_send()
        to_outer.wait_recv()

    @pl.when(span < spans - 1)
    def _():
        to_outer.wait_send()
        to_inner.wait_recv()


def halo(flow, passages, spans):
    stations, rows, cols = flow.shape
    groups = LANES // stations
    chunks = 4
    f32 = jnp.float32
    vmem = pl.BlockSpec(memory_space=pltpu.VMEM)
    return pl.pallas_call(
        functools.partial(halo_kernel, passages, spans, chunks),
        out_shape=(
            jax.ShapeDtypeStruct((2, stations, cols), f32),
            jax.ShapeDtypeStruct((2, rows // groups, LANES), f32),
        ),
        in_specs=[pl.BlockSpec(memory_space=pl.ANY)],
        out_specs=(vmem, vmem),
        scratch_shapes=[
            pltpu.VMEM((stations, rows, LANES), f32),
            pltpu.VMEM((stations, rows, LANES), f32),
            pltpu.VMEM((stations, 8, cols), f32),
            pltpu.VMEM((stations, 8, cols), f32),
            pltpu.VMEM((2, stations, cols), f32),
            pltpu.VMEM((2, rows // groups, LANES), f32),
            pltpu.SemaphoreType.DMA((2 + 2 * chunks,)),
            pltpu.SemaphoreType.DMA((4,)),
            pltpu.SemaphoreType.DMA((4,)),
        ],
        compiler_params=pltpu.CompilerParams(
            collective_id=0, has_side_effects=True, vmem_limit_bytes=24 * MIB),
        name="halo",
    )(flow)


def stencil_kernel(
    planes, plane_index, mode_order, flow, rows_in, cols_in, swirl, diff, modes, basis,
    out, amp, coef_e, coef_w, coef_c, picked, fold, shapes,
):
    block, rows, cols = flow.shape
    stations = rows_in.shape[1]
    per = cols_in.shape[1]
    m = modes.shape[0]
    first = pl.program_id(0) * block

    @pl.when(first == 0)
    def _():
        d = diff[...]
        half = 0.5 * jnp.broadcast_to(swirl[...], (LANES, rows)).T
        half = jnp.concatenate([half] * (cols // LANES), axis=1)
        coef_e[...] = d - half
        coef_w[...] = d + half
        coef_c[...] = 1.0 - 4.0 * d
        for j in range(m):
            picked[pl.ds(j, 1), :] = modes[pl.ds(mode_order[j], 1), :]

    lane = lax.broadcasted_iota(jnp.int32, (8, LANES), 1)
    sub = lax.broadcasted_iota(jnp.int32, (8, cols), 0)
    last = cols - LANES
    for r in range(0, rows, 8):
        part = slice(r, r + 8)
        of_e, of_w, of_c, of_d = coef_e[part, :], coef_w[part, :], coef_c[part, :], diff[part, :]
        for b in range(block):
            z = first + b
            center = flow[b, part, :]
            if r == 0:
                inner = jnp.where(sub == 0, rows_in[0, pl.ds(z, 1), :], pltpu.roll(center, 1, 0))
            else:
                inner = flow[b, r - 1:r + 7, :]
            if r == rows - 8:
                outer = jnp.where(sub == 7, rows_in[1, pl.ds(z, 1), :], pltpu.roll(center, 7, 0))
            else:
                outer = flow[b, r + 1:r + 9, :]
            spot = (r // per) * stations + z
            packed = slice(r % per, r % per + 8)
            west_edge = pltpu.roll(cols_in[0, packed, :], LANES - spot, 1)
            east_edge = pltpu.roll(cols_in[1, packed, :], LANES - 1 - spot, 1)
            east = pltpu.roll(center, cols - 1, 1)
            west = pltpu.roll(center, 1, 1)
            east = jnp.concatenate(
                [east[:, :last], jnp.where(lane == LANES - 1, east_edge, east[:, last:])], axis=1)
            west = jnp.concatenate(
                [jnp.where(lane == 0, west_edge, west[:, :LANES]), west[:, LANES:]], axis=1)
            value = of_c * center + of_e * east + of_w * west + of_d * (outer + inner)
            out[b, part, :] = value
            total = value[:, :PERIOD]
            for c in range(PERIOD, cols, PERIOD):
                total = total + value[:, c:c + PERIOD]
            fold[b, part, :] = total

    for p in range(planes):
        b = plane_index[p] - first

        @pl.when((b >= 0) & (b < block))
        def _():
            shapes[p * m:(p + 1) * m, :] = jnp.dot(
                picked[...], fold[b], precision=lax.Precision.HIGHEST,
                preferred_element_type=jnp.float32)

    @pl.when(first == stations - block)
    def _():
        lines = jnp.dot(
            shapes[...], basis[...], precision=lax.Precision.HIGHEST,
            preferred_element_type=jnp.float32)
        tiles = m // 8
        for p in range(planes):
            for h in range(2):
                at = (2 * p + h) * tiles
                amp[at:at + tiles] = (
                    lines[p * m:(p + 1) * m, h * LANES:(h + 1) * LANES].reshape(tiles, 8, LANES))


def stencil(flow, rows_in, cols_in, swirl, diff, plane_index, modes, mode_order):
    stations, rows, cols = flow.shape
    planes = plane_index.shape[0]
    m = modes.shape[0]
    block = 4
    f32 = jnp.float32
    smem = pl.BlockSpec(memory_space=pltpu.SMEM)
    some = pl.BlockSpec((block, rows, cols), lambda z: (z, 0, 0))

    def whole(shape):
        return pl.BlockSpec(shape, lambda z: (0,) * len(shape))

    tiles = planes * m * 2 * K // (8 * LANES)
    return pl.pallas_call(
        functools.partial(stencil_kernel, planes),
        out_shape=(
            jax.ShapeDtypeStruct(flow.shape, f32),
            jax.ShapeDtypeStruct((tiles, 8, LANES), f32),
        ),
        grid=(stations // block,),
        in_specs=[
            smem, smem, some, whole(rows_in.shape), whole(cols_in.shape), whole((1, rows)),
            whole(diff.shape), whole(modes.shape), whole((PERIOD, 2 * K)),
        ],
        out_specs=(some, whole((tiles, 8, LANES))),
        scratch_shapes=[
            pltpu.VMEM((rows, cols), f32),
            pltpu.VMEM((rows, cols), f32),
            pltpu.VMEM((rows, cols), f32),
            pltpu.VMEM((m, rows), f32),
            pltpu.VMEM((block, rows, PERIOD), f32),
            pltpu.VMEM((planes * m, PERIOD), f32),
        ],
        compiler_params=pltpu.CompilerParams(vmem_limit_bytes=40 * MIB),
        name="stencil",
    )(plane_index, mode_order, flow, rows_in, cols_in, swirl.reshape(1, rows), diff, modes,
      jnp.asarray(dft_basis()))


def sum_kernel(sizes, amp, out, acc, full, *rest):
    recvs, (send_sem, recv_sem, send_sem2, recv_sem2) = rest[:3], rest[3:]
    cores, xs, zs = sizes
    span = lax.axis_index("span")
    core, x, z = lax.rem(span, cores), span // cores, lax.axis_index("passage")
    mine = (core, x, z)

    def peer(s, k):
        if s == 0:
            return {"span": x * cores + k}
        if s == 1:
            return {"span": k * cores + core}
        return {"passage": k}

    def others(s):
        return [(d, lax.rem(mine[s] + d, sizes[s])) for d in range(1, sizes[s])]

    barrier = pltpu.get_barrier_semaphore()
    for s in range(3):
        for _, k in others(s):
            pl.semaphore_signal(barrier, inc=1, device_id=peer(s, k), device_id_type=MESH)
    pl.semaphore_wait(barrier, sum(sizes) - 3)

    size = amp.shape[0]
    base = 0
    bases, widths = [], []
    index = 0
    firsts = []
    for s in range(3):
        width = size // sizes[s]
        source = amp if s == 0 else acc
        firsts.append(index)
        copies = []
        for d, k in others(s):
            copy = pltpu.make_async_remote_copy(
                src_ref=source.at[pl.ds(base + k * width, width)], dst_ref=recvs[s].at[d - 1],
                send_sem=send_sem.at[index], recv_sem=recv_sem.at[index],
                device_id=peer(s, k), device_id_type=MESH)
            copy.start()
            copies.append(copy)
            index += 1
        base = base + mine[s] * width
        size = width
        bases.append(base)
        widths.append(width)
        for copy in copies:
            copy.wait()
        part = pl.ds(base, width)
        total = source[part]
        for d in range(1, sizes[s]):
            total = total + recvs[s][d - 1]
        if s < 2:
            acc[part] = total
        else:
            full[part] = total

    for s in (2, 1, 0):
        part = pl.ds(bases[s], widths[s])
        copies = []
        for d, k in others(s):
            at = firsts[s] + d - 1
            copy = pltpu.make_async_remote_copy(
                src_ref=full.at[part], dst_ref=full.at[part],
                send_sem=send_sem2.at[at], recv_sem=recv_sem2.at[at],
                device_id=peer(s, k), device_id_type=MESH)
            copy.start()
            copies.append(copy)
        for copy in copies:
            copy.wait()

    planes, m, _ = out.shape
    tiles = m // 8
    for p in range(planes):
        for h in range(2):
            out[p, :, h * LANES:(h + 1) * LANES] = (
                full[pl.ds((2 * p + h) * tiles, tiles)].reshape(m, LANES))


def amplitude_sum(amp, planes, m, sizes):
    f32 = jnp.float32
    tiles = amp.shape[0]
    widths = [tiles // math.prod(sizes[:s + 1]) for s in range(3)]
    total = sum(sizes) - 3
    vmem = pl.BlockSpec(memory_space=pltpu.VMEM)
    return pl.pallas_call(
        functools.partial(sum_kernel, sizes),
        out_shape=jax.ShapeDtypeStruct((planes, m, 2 * K), f32),
        in_specs=[vmem],
        out_specs=vmem,
        scratch_shapes=[
            pltpu.VMEM((tiles, 8, LANES), f32),
            pltpu.VMEM((tiles, 8, LANES), f32),
            *[pltpu.VMEM((max(n - 1, 1), w, 8, LANES), f32) for n, w in zip(sizes, widths)],
            *[pltpu.SemaphoreType.DMA((total,)) for _ in range(4)],
        ],
        compiler_params=pltpu.CompilerParams(
            collective_id=1, has_side_effects=True, vmem_limit_bytes=16 * MIB),
        name="amplitude_sum",
    )(amp)


def body(passages, spans, flow_state, swirl_speed, diffusivity, plane_index, radial_modes, mode_order):
    rows_in, cols_in = halo(flow_state, passages, spans)
    next_state, partial_value = stencil(
        flow_state, rows_in, cols_in, swirl_speed, diffusivity, plane_index, radial_modes, mode_order)
    sizes = (2, spans // 2, passages)
    amplitudes = amplitude_sum(partial_value, plane_index.shape[0], mode_order.shape[0], sizes)
    return (next_state, amplitudes)


def solution(mesh):
    return jax.shard_map(
        functools.partial(body, mesh.shape["passage"], mesh.shape["span"]),
        mesh=mesh,
        in_specs=(
            P("group", "span", "passage"),
            P(("group", "span")),
            P(("group", "span"), "passage"),
            P("group"),
            P(None, "span"),
            P(),
        ),
        out_specs=(P("group", "span", "passage"), P("group", None, None)),
        check_vma=False,
    )
```

```python
import functools
import math

import jax
import jax.numpy as jnp
import numpy as np
from jax import lax
from jax.experimental import pallas as pl
from jax.experimental.pallas import tpu as pltpu
from jax.sharding import PartitionSpec as P

NTH = 4096
BLADES = 16
K = 128
PERIOD = NTH // BLADES
LANES = 128
MIB = 1024 * 1024
MESH = pl.DeviceIdType.MESH


def dft_basis():
    t = np.arange(PERIOD)[:, None]
    k = np.arange(K)[None, :]
    angles = (t * k % PERIOD) * (2.0 * math.pi / PERIOD)
    both = np.concatenate([np.cos(angles), -np.sin(angles)], axis=1)
    return (both / math.sqrt(NTH)).astype(np.float32)


def halo_kernel(
    passages, spans, chunks, flow, rows_out, cols_out,
    left, right, low, high, rows_send, cols_send, load_sem, send_sem, recv_sem,
):
    stations, rows, cols = flow.shape
    passage = lax.axis_index("passage")
    span = lax.axis_index("span")
    groups = LANES // stations
    per = rows // groups
    step = stations // chunks

    def loads(c):
        part = pl.ds(c * step, step)
        return [
            pltpu.make_async_copy(
                flow.at[part, :, pl.ds(0, LANES)], left.at[part], load_sem.at[2 + 2 * c]),
            pltpu.make_async_copy(
                flow.at[part, :, pl.ds(cols - LANES, LANES)], right.at[part],
                load_sem.at[3 + 2 * c]),
        ]

    row_loads = [
        pltpu.make_async_copy(flow.at[:, pl.ds(0, 8), :], low, load_sem.at[0]),
        pltpu.make_async_copy(flow.at[:, pl.ds(rows - 8, 8), :], high, load_sem.at[1]),
    ]
    for copy in row_loads:
        copy.start()
    for c in range(chunks):
        for copy in loads(c):
            copy.start()

    west = lax.rem(passage + passages - 1, passages)
    east = lax.rem(passage + 1, passages)
    outer = jnp.minimum(span + 1, spans - 1)
    inner = jnp.maximum(span - 1, 0)
    barrier = pltpu.get_barrier_semaphore()
    for side in (west, east):
        pl.semaphore_signal(barrier, inc=1, device_id={"passage": side}, device_id_type=MESH)
    for side in (1, spans - 1):
        pl.semaphore_signal(
            barrier, inc=1, device_id={"span": lax.rem(span + side, spans)}, device_id_type=MESH)
    pl.semaphore_wait(barrier, 4)

    to_inner = pltpu.make_async_remote_copy(
        src_ref=rows_send.at[0], dst_ref=rows_out.at[1], send_sem=send_sem.at[0],
        recv_sem=recv_sem.at[0], device_id={"span": inner}, device_id_type=MESH)
    to_outer = pltpu.make_async_remote_copy(
        src_ref=rows_send.at[1], dst_ref=rows_out.at[0], send_sem=send_sem.at[1],
        recv_sem=recv_sem.at[1], device_id={"span": outer}, device_id_type=MESH)
    to_west = pltpu.make_async_remote_copy(
        src_ref=cols_send.at[0], dst_ref=cols_out.at[1], send_sem=send_sem.at[2],
        recv_sem=recv_sem.at[2], device_id={"passage": west}, device_id_type=MESH)
    to_east = pltpu.make_async_remote_copy(
        src_ref=cols_send.at[1], dst_ref=cols_out.at[0], send_sem=send_sem.at[3],
        recv_sem=recv_sem.at[3], device_id={"passage": east}, device_id_type=MESH)

    for copy in row_loads:
        copy.wait()
    rows_send[0] = low[:, 0, :]
    rows_send[1] = high[:, 7, :]

    @pl.when(span > 0)
    def _():
        to_inner.start()

    @pl.when(span < spans - 1)
    def _():
        to_outer.start()

    @pl.when(span == 0)
    def _():
        rows_out[0] = jnp.zeros((stations, cols), jnp.float32)

    @pl.when(span == spans - 1)
    def _():
        rows_out[1] = jnp.zeros((stations, cols), jnp.float32)

    lane = lax.broadcasted_iota(jnp.int32, (per, LANES), 1)

    def pack(i, carry):
        a, b = carry
        for z, g in [(4 * i + j, g) for j in range(4) for g in range(groups)]:
            spot = g * stations + z
            part = pl.ds(g * per, per)
            a = jnp.where(lane == spot, pltpu.roll(left[z, part, :], spot, 1), a)
            b = jnp.where(lane == spot, pltpu.roll(right[z, part, :], spot + 1, 1), b)
        return a, b

    zero = jnp.zeros((per, LANES), jnp.float32)
    carry = (zero, zero)
    for c in range(chunks):
        for copy in loads(c):
            copy.wait()
        carry = lax.fori_loop(c * step // 4, (c + 1) * step // 4, pack, carry)
    cols_send[0], cols_send[1] = carry
    to_west.start()
    to_east.start()
    to_west.wait()
    to_east.wait()

    @pl.when(span > 0)
    def _():
        to_inner.wait_send()
        to_outer.wait_recv()

    @pl.when(span < spans - 1)
    def _():
        to_outer.wait_send()
        to_inner.wait_recv()


def halo(flow, passages, spans):
    stations, rows, cols = flow.shape
    groups = LANES // stations
    chunks = 4
    f32 = jnp.float32
    vmem = pl.BlockSpec(memory_space=pltpu.VMEM)
    return pl.pallas_call(
        functools.partial(halo_kernel, passages, spans, chunks),
        out_shape=(
            jax.ShapeDtypeStruct((2, stations, cols), f32),
            jax.ShapeDtypeStruct((2, rows // groups, LANES), f32),
        ),
        in_specs=[pl.BlockSpec(memory_space=pl.ANY)],
        out_specs=(vmem, vmem),
        scratch_shapes=[
            pltpu.VMEM((stations, rows, LANES), f32),
            pltpu.VMEM((stations, rows, LANES), f32),
            pltpu.VMEM((stations, 8, cols), f32),
            pltpu.VMEM((stations, 8, cols), f32),
            pltpu.VMEM((2, stations, cols), f32),
            pltpu.VMEM((2, rows // groups, LANES), f32),
            pltpu.SemaphoreType.DMA((2 + 2 * chunks,)),
            pltpu.SemaphoreType.DMA((4,)),
            pltpu.SemaphoreType.DMA((4,)),
        ],
        compiler_params=pltpu.CompilerParams(
            collective_id=0, has_side_effects=True, vmem_limit_bytes=24 * MIB),
        name="halo",
    )(flow)


def stencil_kernel(
    planes, plane_index, mode_order, flow, rows_in, cols_in, swirl, diff, modes, basis,
    out, amp, coef_e, coef_w, coef_c, picked, fold, shapes,
):
    block, rows, cols = flow.shape
    stations = rows_in.shape[1]
    per = cols_in.shape[1]
    m = modes.shape[0]
    first = pl.program_id(0) * block

    @pl.when(first == 0)
    def _():
        d = diff[...]
        half = 0.5 * jnp.broadcast_to(swirl[...], (LANES, rows)).T
        half = jnp.concatenate([half] * (cols // LANES), axis=1)
        coef_e[...] = d - half
        coef_w[...] = d + half
        coef_c[...] = 1.0 - 4.0 * d
        for j in range(m):
            picked[pl.ds(j, 1), :] = modes[pl.ds(mode_order[j], 1), :]

    lane = lax.broadcasted_iota(jnp.int32, (8, LANES), 1)
    sub = lax.broadcasted_iota(jnp.int32, (8, cols), 0)
    last = cols - LANES
    for r in range(0, rows, 8):
        part = slice(r, r + 8)
        of_e, of_w, of_c, of_d = coef_e[part, :], coef_w[part, :], coef_c[part, :], diff[part, :]
        for b in range(block):
            z = first + b
            center = flow[b, part, :]
            if r == 0:
                inner = jnp.where(sub == 0, rows_in[0, pl.ds(z, 1), :], pltpu.roll(center, 1, 0))
            else:
                inner = flow[b, r - 1:r + 7, :]
            if r == rows - 8:
                outer = jnp.where(sub == 7, rows_in[1, pl.ds(z, 1), :], pltpu.roll(center, 7, 0))
            else:
                outer = flow[b, r + 1:r + 9, :]
            spot = (r // per) * stations + z
            packed = slice(r % per, r % per + 8)
            west_edge = pltpu.roll(cols_in[0, packed, :], LANES - spot, 1)
            east_edge = pltpu.roll(cols_in[1, packed, :], LANES - 1 - spot, 1)
            east = pltpu.roll(center, cols - 1, 1)
            west = pltpu.roll(center, 1, 1)
            east = jnp.concatenate(
                [east[:, :last], jnp.where(lane == LANES - 1, east_edge, east[:, last:])], axis=1)
            west = jnp.concatenate(
                [jnp.where(lane == 0, west_edge, west[:, :LANES]), west[:, LANES:]], axis=1)
            value = of_c * center + of_e * east + of_w * west + of_d * (outer + inner)
            out[b, part, :] = value
            total = value[:, :PERIOD]
            for c in range(PERIOD, cols, PERIOD):
                total = total + value[:, c:c + PERIOD]
            fold[b, part, :] = total

    for p in range(planes):
        b = plane_index[p] - first

        @pl.when((b >= 0) & (b < block))
        def _():
            shapes[p * m:(p + 1) * m, :] = jnp.dot(
                picked[...], fold[b], precision=lax.Precision.HIGHEST,
                preferred_element_type=jnp.float32)

    @pl.when(first == stations - block)
    def _():
        lines = jnp.dot(
            shapes[...], basis[...], precision=lax.Precision.HIGHEST,
            preferred_element_type=jnp.float32)
        tiles = m // 8
        for p in range(planes):
            for h in range(2):
                at = (2 * p + h) * tiles
                amp[at:at + tiles] = (
                    lines[p * m:(p + 1) * m, h * LANES:(h + 1) * LANES].reshape(tiles, 8, LANES))


def stencil(flow, rows_in, cols_in, swirl, diff, plane_index, modes, mode_order):
    stations, rows, cols = flow.shape
    planes = plane_index.shape[0]
    m = modes.shape[0]
    block = 4
    f32 = jnp.float32
    smem = pl.BlockSpec(memory_space=pltpu.SMEM)
    some = pl.BlockSpec((block, rows, cols), lambda z: (z, 0, 0))

    def whole(shape):
        return pl.BlockSpec(shape, lambda z: (0,) * len(shape))

    tiles = planes * m * 2 * K // (8 * LANES)
    return pl.pallas_call(
        functools.partial(stencil_kernel, planes),
        out_shape=(
            jax.ShapeDtypeStruct(flow.shape, f32),
            jax.ShapeDtypeStruct((tiles, 8, LANES), f32),
        ),
        grid=(stations // block,),
        in_specs=[
            smem, smem, some, whole(rows_in.shape), whole(cols_in.shape), whole((1, rows)),
            whole(diff.shape), whole(modes.shape), whole((PERIOD, 2 * K)),
        ],
        out_specs=(some, whole((tiles, 8, LANES))),
        scratch_shapes=[
            pltpu.VMEM((rows, cols), f32),
            pltpu.VMEM((rows, cols), f32),
            pltpu.VMEM((rows, cols), f32),
            pltpu.VMEM((m, rows), f32),
            pltpu.VMEM((block, rows, PERIOD), f32),
            pltpu.VMEM((planes * m, PERIOD), f32),
        ],
        compiler_params=pltpu.CompilerParams(vmem_limit_bytes=40 * MIB),
        name="stencil",
    )(plane_index, mode_order, flow, rows_in, cols_in, swirl.reshape(1, rows), diff, modes,
      jnp.asarray(dft_basis()))


def sum_kernel(sizes, jobs, amp, out, acc, full, *rest):
    recvs, (send_sem, recv_sem, send_sem2, recv_sem2) = rest[:3], rest[3:]
    cores, xs, zs = sizes
    span = lax.axis_index("span")
    core, x, z = lax.rem(span, cores), span // cores, lax.axis_index("passage")
    mine = (core, x, z)

    def peer(s, k):
        if s == 0:
            return {"span": x * cores + k}
        if s == 1:
            return {"span": k * cores + core}
        return {"passage": k}

    def others(s):
        return [(d, lax.rem(mine[s] + d, sizes[s])) for d in range(1, sizes[s])]

    barrier = pltpu.get_barrier_semaphore()
    for s in range(3):
        for _, k in others(s):
            pl.semaphore_signal(barrier, inc=1, device_id=peer(s, k), device_id_type=MESH)
    pl.semaphore_wait(barrier, sum(sizes) - 3)

    tiles = amp.shape[0] // jobs
    each = sum(sizes) - 3

    class Job:
        def __init__(self, number):
            self.order = (0, 1, 2) if number % 2 == 0 else (0, 2, 1)
            self.number = number
            self.base, self.size = number * tiles, tiles
            self.parts = []
            self.copies = []

        def at(self, s, d):
            return self.number * each + sum(sizes[:s]) - s + d - 1

        def start(self, step):
            gather = step >= 3
            s = self.order[5 - step if gather else step]
            width = self.size // sizes[s]
            self.copies = []
            for d, k in others(s):
                n = self.at(s, d)
                if gather:
                    part = self.parts[5 - step]
                    source, target = full.at[part], full.at[part]
                    sems = (send_sem2.at[n], recv_sem2.at[n])
                else:
                    source = (amp if step == 0 else acc).at[pl.ds(self.base + k * width, width)]
                    target = recvs[s].at[self.number, d - 1, pl.ds(0, width)]
                    sems = (send_sem.at[n], recv_sem.at[n])
                copy = pltpu.make_async_remote_copy(
                    src_ref=source, dst_ref=target, send_sem=sems[0], recv_sem=sems[1],
                    device_id=peer(s, k), device_id_type=MESH)
                copy.start()
                self.copies.append(copy)

        def finish(self, step):
            for copy in self.copies:
                copy.wait()
            if step >= 3:
                return
            s = self.order[step]
            width = self.size // sizes[s]
            self.base, self.size = self.base + mine[s] * width, width
            part = pl.ds(self.base, width)
            self.parts.append(part)
            total = (amp if step == 0 else acc)[part]
            for d in range(1, sizes[s]):
                total = total + recvs[s][self.number, d - 1, :width]
            (acc if step < 2 else full)[part] = total

    work = [Job(number) for number in range(jobs)]
    for job in work:
        job.start(0)
    for step in range(6):
        for job in work:
            job.finish(step)
            if step < 5:
                job.start(step + 1)

    planes, m, _ = out.shape
    tiles = m // 8
    for p in range(planes):
        for h in range(2):
            out[p, :, h * LANES:(h + 1) * LANES] = (
                full[pl.ds((2 * p + h) * tiles, tiles)].reshape(m, LANES))


def amplitude_sum(amp, planes, m, sizes):
    f32 = jnp.float32
    tiles = amp.shape[0]
    jobs = 4 if tiles % (4 * math.prod(sizes)) == 0 else 1
    cores, xs, zs = sizes
    widths = [tiles // jobs // n for n in (cores, cores * xs, cores * zs)]
    total = sum(sizes) - 3
    vmem = pl.BlockSpec(memory_space=pltpu.VMEM)
    return pl.pallas_call(
        functools.partial(sum_kernel, sizes, jobs),
        out_shape=jax.ShapeDtypeStruct((planes, m, 2 * K), f32),
        in_specs=[vmem],
        out_specs=vmem,
        scratch_shapes=[
            pltpu.VMEM((tiles, 8, LANES), f32),
            pltpu.VMEM((tiles, 8, LANES), f32),
            *[pltpu.VMEM((jobs, max(n - 1, 1), w, 8, LANES), f32) for n, w in zip(sizes, widths)],
            *[pltpu.SemaphoreType.DMA((jobs * total,)) for _ in range(4)],
        ],
        compiler_params=pltpu.CompilerParams(
            collective_id=1, has_side_effects=True, vmem_limit_bytes=16 * MIB),
        name="amplitude_sum",
    )(amp)


def body(passages, spans, flow_state, swirl_speed, diffusivity, plane_index, radial_modes, mode_order):
    rows_in, cols_in = halo(flow_state, passages, spans)
    next_state, partial_value = stencil(
        flow_state, rows_in, cols_in, swirl_speed, diffusivity, plane_index, radial_modes, mode_order)
    sizes = (2, spans // 2, passages)
    amplitudes = amplitude_sum(partial_value, plane_index.shape[0], mode_order.shape[0], sizes)
    return (next_state, amplitudes)


def solution(mesh):
    return jax.shard_map(
        functools.partial(body, mesh.shape["passage"], mesh.shape["span"]),
        mesh=mesh,
        in_specs=(
            P("group", "span", "passage"),
            P(("group", "span")),
            P(("group", "span"), "passage"),
            P("group"),
            P(None, "span"),
            P(),
        ),
        out_specs=(P("group", "span", "passage"), P("group", None, None)),
        check_vma=False,
    )
```

```python
import functools
import math

import jax
import jax.numpy as jnp
import numpy as np
from jax import lax
from jax.experimental import pallas as pl
from jax.experimental.pallas import tpu as pltpu
from jax.sharding import PartitionSpec as P

NTH = 4096
BLADES = 16
K = 128
PERIOD = NTH // BLADES
LANES = 128
MIB = 1024 * 1024
MESH = pl.DeviceIdType.MESH


def dft_basis():
    t = np.arange(PERIOD)[:, None]
    k = np.arange(K)[None, :]
    angles = (t * k % PERIOD) * (2.0 * math.pi / PERIOD)
    both = np.concatenate([np.cos(angles), -np.sin(angles)], axis=1)
    return (both / math.sqrt(NTH)).astype(np.float32)


def halo_kernel(
    passages, spans, chunks, flow, rows_out, cols_out,
    left, right, low, high, rows_send, cols_send, load_sem, send_sem, recv_sem,
):
    stations, rows, cols = flow.shape
    passage = lax.axis_index("passage")
    span = lax.axis_index("span")
    groups = LANES // stations
    per = rows // groups
    step = stations // chunks

    def loads(c):
        part = pl.ds(c * step, step)
        return [
            pltpu.make_async_copy(
                flow.at[part, :, pl.ds(0, LANES)], left.at[part], load_sem.at[2 + 2 * c]),
            pltpu.make_async_copy(
                flow.at[part, :, pl.ds(cols - LANES, LANES)], right.at[part],
                load_sem.at[3 + 2 * c]),
        ]

    row_loads = [
        pltpu.make_async_copy(flow.at[:, pl.ds(0, 8), :], low, load_sem.at[0]),
        pltpu.make_async_copy(flow.at[:, pl.ds(rows - 8, 8), :], high, load_sem.at[1]),
    ]
    for copy in row_loads:
        copy.start()
    for c in range(chunks):
        for copy in loads(c):
            copy.start()

    west = lax.rem(passage + passages - 1, passages)
    east = lax.rem(passage + 1, passages)
    outer = jnp.minimum(span + 1, spans - 1)
    inner = jnp.maximum(span - 1, 0)
    barrier = pltpu.get_barrier_semaphore()
    for side in (west, east):
        pl.semaphore_signal(barrier, inc=1, device_id={"passage": side}, device_id_type=MESH)
    for side in (1, spans - 1):
        pl.semaphore_signal(
            barrier, inc=1, device_id={"span": lax.rem(span + side, spans)}, device_id_type=MESH)
    pl.semaphore_wait(barrier, 4)

    to_inner = pltpu.make_async_remote_copy(
        src_ref=rows_send.at[0], dst_ref=rows_out.at[1], send_sem=send_sem.at[0],
        recv_sem=recv_sem.at[0], device_id={"span": inner}, device_id_type=MESH)
    to_outer = pltpu.make_async_remote_copy(
        src_ref=rows_send.at[1], dst_ref=rows_out.at[0], send_sem=send_sem.at[1],
        recv_sem=recv_sem.at[1], device_id={"span": outer}, device_id_type=MESH)
    to_west = pltpu.make_async_remote_copy(
        src_ref=cols_send.at[0], dst_ref=cols_out.at[1], send_sem=send_sem.at[2],
        recv_sem=recv_sem.at[2], device_id={"passage": west}, device_id_type=MESH)
    to_east = pltpu.make_async_remote_copy(
        src_ref=cols_send.at[1], dst_ref=cols_out.at[0], send_sem=send_sem.at[3],
        recv_sem=recv_sem.at[3], device_id={"passage": east}, device_id_type=MESH)

    for copy in row_loads:
        copy.wait()
    rows_send[0] = low[:, 0, :]
    rows_send[1] = high[:, 7, :]

    @pl.when(span > 0)
    def _():
        to_inner.start()

    @pl.when(span < spans - 1)
    def _():
        to_outer.start()

    @pl.when(span == 0)
    def _():
        rows_out[0] = jnp.zeros((stations, cols), jnp.float32)

    @pl.when(span == spans - 1)
    def _():
        rows_out[1] = jnp.zeros((stations, cols), jnp.float32)

    lane = lax.broadcasted_iota(jnp.int32, (per, LANES), 1)

    def pack(i, carry):
        a, b = carry
        for z, g in [(step * i + j, g) for j in range(step) for g in range(groups)]:
            spot = g * stations + z
            part = pl.ds(g * per, per)
            a = jnp.where(lane == spot, pltpu.roll(left[z, part, :], spot, 1), a)
            b = jnp.where(lane == spot, pltpu.roll(right[z, part, :], spot + 1, 1), b)
        return a, b

    zero = jnp.zeros((per, LANES), jnp.float32)
    carry = (zero, zero)
    for c in range(chunks):
        for copy in loads(c):
            copy.wait()
        carry = pack(c, carry)
    cols_send[0], cols_send[1] = carry
    to_west.start()
    to_east.start()
    to_west.wait()
    to_east.wait()

    @pl.when(span > 0)
    def _():
        to_inner.wait_send()
        to_outer.wait_recv()

    @pl.when(span < spans - 1)
    def _():
        to_outer.wait_send()
        to_inner.wait_recv()


def halo(flow, passages, spans):
    stations, rows, cols = flow.shape
    groups = LANES // stations
    chunks = 4
    f32 = jnp.float32
    vmem = pl.BlockSpec(memory_space=pltpu.VMEM)
    return pl.pallas_call(
        functools.partial(halo_kernel, passages, spans, chunks),
        out_shape=(
            jax.ShapeDtypeStruct((2, stations, cols), f32),
            jax.ShapeDtypeStruct((2, rows // groups, LANES), f32),
        ),
        in_specs=[pl.BlockSpec(memory_space=pl.ANY)],
        out_specs=(vmem, vmem),
        scratch_shapes=[
            pltpu.VMEM((stations, rows, LANES), f32),
            pltpu.VMEM((stations, rows, LANES), f32),
            pltpu.VMEM((stations, 8, cols), f32),
            pltpu.VMEM((stations, 8, cols), f32),
            pltpu.VMEM((2, stations, cols), f32),
            pltpu.VMEM((2, rows // groups, LANES), f32),
            pltpu.SemaphoreType.DMA((2 + 2 * chunks,)),
            pltpu.SemaphoreType.DMA((4,)),
            pltpu.SemaphoreType.DMA((4,)),
        ],
        compiler_params=pltpu.CompilerParams(
            collective_id=0, has_side_effects=True, vmem_limit_bytes=24 * MIB),
        name="halo",
    )(flow)


def stencil_kernel(
    planes, plane_index, mode_order, flow, rows_in, cols_in, swirl, diff, modes, basis,
    out, amp, coef_e, coef_w, coef_c, picked, fold, shapes,
):
    block, rows, cols = flow.shape
    stations = rows_in.shape[1]
    per = cols_in.shape[1]
    m = modes.shape[0]
    first = pl.program_id(0) * block

    @pl.when(first == 0)
    def _():
        d = diff[...]
        half = 0.5 * jnp.broadcast_to(swirl[...], (LANES, rows)).T
        half = jnp.concatenate([half] * (cols // LANES), axis=1)
        coef_e[...] = d - half
        coef_w[...] = d + half
        coef_c[...] = 1.0 - 4.0 * d
        for j in range(m):
            picked[pl.ds(j, 1), :] = modes[pl.ds(mode_order[j], 1), :]

    lane = lax.broadcasted_iota(jnp.int32, (8, LANES), 1)
    sub = lax.broadcasted_iota(jnp.int32, (8, cols), 0)
    last = cols - LANES
    for r in range(0, rows, 8):
        part = slice(r, r + 8)
        of_e, of_w, of_c, of_d = coef_e[part, :], coef_w[part, :], coef_c[part, :], diff[part, :]
        for b in range(block):
            z = first + b
            center = flow[b, part, :]
            if r == 0:
                inner = jnp.where(sub == 0, rows_in[0, pl.ds(z, 1), :], pltpu.roll(center, 1, 0))
            else:
                inner = flow[b, r - 1:r + 7, :]
            if r == rows - 8:
                outer = jnp.where(sub == 7, rows_in[1, pl.ds(z, 1), :], pltpu.roll(center, 7, 0))
            else:
                outer = flow[b, r + 1:r + 9, :]
            spot = (r // per) * stations + z
            packed = slice(r % per, r % per + 8)
            west_edge = pltpu.roll(cols_in[0, packed, :], LANES - spot, 1)
            east_edge = pltpu.roll(cols_in[1, packed, :], LANES - 1 - spot, 1)
            east = pltpu.roll(center, cols - 1, 1)
            west = pltpu.roll(center, 1, 1)
            east = jnp.concatenate(
                [east[:, :last], jnp.where(lane == LANES - 1, east_edge, east[:, last:])], axis=1)
            west = jnp.concatenate(
                [jnp.where(lane == 0, west_edge, west[:, :LANES]), west[:, LANES:]], axis=1)
            value = of_c * center + of_e * east + of_w * west + of_d * (outer + inner)
            out[b, part, :] = value
            total = value[:, :PERIOD]
            for c in range(PERIOD, cols, PERIOD):
                total = total + value[:, c:c + PERIOD]
            fold[b, part, :] = total

    for p in range(planes):
        b = plane_index[p] - first

        @pl.when((b >= 0) & (b < block))
        def _():
            shapes[p * m:(p + 1) * m, :] = jnp.dot(
                picked[...], fold[b], precision=lax.Precision.HIGHEST,
                preferred_element_type=jnp.float32)

    @pl.when(first == stations - block)
    def _():
        lines = jnp.dot(
            shapes[...], basis[...], precision=lax.Precision.HIGHEST,
            preferred_element_type=jnp.float32)
        tiles = m // 8
        for p in range(planes):
            for h in range(2):
                at = (2 * p + h) * tiles
                amp[at:at + tiles] = (
                    lines[p * m:(p + 1) * m, h * LANES:(h + 1) * LANES].reshape(tiles, 8, LANES))


def stencil(flow, rows_in, cols_in, swirl, diff, plane_index, modes, mode_order):
    stations, rows, cols = flow.shape
    planes = plane_index.shape[0]
    m = modes.shape[0]
    block = 4
    f32 = jnp.float32
    smem = pl.BlockSpec(memory_space=pltpu.SMEM)
    some = pl.BlockSpec((block, rows, cols), lambda z: (z, 0, 0))

    def whole(shape):
        return pl.BlockSpec(shape, lambda z: (0,) * len(shape))

    tiles = planes * m * 2 * K // (8 * LANES)
    return pl.pallas_call(
        functools.partial(stencil_kernel, planes),
        out_shape=(
            jax.ShapeDtypeStruct(flow.shape, f32),
            jax.ShapeDtypeStruct((tiles, 8, LANES), f32),
        ),
        grid=(stations // block,),
        in_specs=[
            smem, smem, some, whole(rows_in.shape), whole(cols_in.shape), whole((1, rows)),
            whole(diff.shape), whole(modes.shape), whole((PERIOD, 2 * K)),
        ],
        out_specs=(some, whole((tiles, 8, LANES))),
        scratch_shapes=[
            pltpu.VMEM((rows, cols), f32),
            pltpu.VMEM((rows, cols), f32),
            pltpu.VMEM((rows, cols), f32),
            pltpu.VMEM((m, rows), f32),
            pltpu.VMEM((block, rows, PERIOD), f32),
            pltpu.VMEM((planes * m, PERIOD), f32),
        ],
        compiler_params=pltpu.CompilerParams(vmem_limit_bytes=40 * MIB),
        name="stencil",
    )(plane_index, mode_order, flow, rows_in, cols_in, swirl.reshape(1, rows), diff, modes,
      jnp.asarray(dft_basis()))


def sum_kernel(sizes, jobs, amp, out, acc, full, *rest):
    recvs, (send_sem, recv_sem, send_sem2, recv_sem2) = rest[:3], rest[3:]
    cores, xs, zs = sizes
    span = lax.axis_index("span")
    core, x, z = lax.rem(span, cores), span // cores, lax.axis_index("passage")
    mine = (core, x, z)

    def peer(s, k):
        if s == 0:
            return {"span": x * cores + k}
        if s == 1:
            return {"span": k * cores + core}
        return {"passage": k}

    def others(s):
        return [(d, lax.rem(mine[s] + d, sizes[s])) for d in range(1, sizes[s])]

    barrier = pltpu.get_barrier_semaphore()
    for s in range(3):
        for _, k in others(s):
            pl.semaphore_signal(barrier, inc=1, device_id=peer(s, k), device_id_type=MESH)
    pl.semaphore_wait(barrier, sum(sizes) - 3)

    tiles = amp.shape[0] // jobs
    each = sum(sizes) - 3

    class Job:
        def __init__(self, number):
            self.order = (0, 1, 2) if number % 2 == 0 else (0, 2, 1)
            self.number = number
            self.base, self.size = number * tiles, tiles
            self.parts = []
            self.copies = []

        def at(self, s, d):
            return self.number * each + sum(sizes[:s]) - s + d - 1

        def start(self, step):
            gather = step >= 3
            s = self.order[5 - step if gather else step]
            width = self.size // sizes[s]
            self.copies = []
            for d, k in others(s):
                n = self.at(s, d)
                if gather:
                    part = self.parts[5 - step]
                    source, target = full.at[part], full.at[part]
                    sems = (send_sem2.at[n], recv_sem2.at[n])
                else:
                    source = (amp if step == 0 else acc).at[pl.ds(self.base + k * width, width)]
                    target = recvs[s].at[self.number, d - 1, pl.ds(0, width)]
                    sems = (send_sem.at[n], recv_sem.at[n])
                copy = pltpu.make_async_remote_copy(
                    src_ref=source, dst_ref=target, send_sem=sems[0], recv_sem=sems[1],
                    device_id=peer(s, k), device_id_type=MESH)
                copy.start()
                self.copies.append(copy)

        def finish(self, step):
            for copy in self.copies:
                copy.wait()
            if step >= 3:
                return
            s = self.order[step]
            width = self.size // sizes[s]
            self.base, self.size = self.base + mine[s] * width, width
            part = pl.ds(self.base, width)
            self.parts.append(part)
            total = (amp if step == 0 else acc)[part]
            for d in range(1, sizes[s]):
                total = total + recvs[s][self.number, d - 1, :width]
            (acc if step < 2 else full)[part] = total

    work = [Job(number) for number in range(jobs)]
    for job in work:
        job.start(0)
    for step in range(6):
        for job in work:
            job.finish(step)
            if step < 5:
                job.start(step + 1)

    planes, m, _ = out.shape
    tiles = m // 8
    for p in range(planes):
        for h in range(2):
            out[p, :, h * LANES:(h + 1) * LANES] = (
                full[pl.ds((2 * p + h) * tiles, tiles)].reshape(m, LANES))


def amplitude_sum(amp, planes, m, sizes):
    f32 = jnp.float32
    tiles = amp.shape[0]
    jobs = 4 if tiles % (4 * math.prod(sizes)) == 0 else 1
    cores, xs, zs = sizes
    widths = [tiles // jobs // n for n in (cores, cores * xs, cores * zs)]
    total = sum(sizes) - 3
    vmem = pl.BlockSpec(memory_space=pltpu.VMEM)
    return pl.pallas_call(
        functools.partial(sum_kernel, sizes, jobs),
        out_shape=jax.ShapeDtypeStruct((planes, m, 2 * K), f32),
        in_specs=[vmem],
        out_specs=vmem,
        scratch_shapes=[
            pltpu.VMEM((tiles, 8, LANES), f32),
            pltpu.VMEM((tiles, 8, LANES), f32),
            *[pltpu.VMEM((jobs, max(n - 1, 1), w, 8, LANES), f32) for n, w in zip(sizes, widths)],
            *[pltpu.SemaphoreType.DMA((jobs * total,)) for _ in range(4)],
        ],
        compiler_params=pltpu.CompilerParams(
            collective_id=1, has_side_effects=True, vmem_limit_bytes=16 * MIB),
        name="amplitude_sum",
    )(amp)


def body(passages, spans, flow_state, swirl_speed, diffusivity, plane_index, radial_modes, mode_order):
    rows_in, cols_in = halo(flow_state, passages, spans)
    next_state, partial_value = stencil(
        flow_state, rows_in, cols_in, swirl_speed, diffusivity, plane_index, radial_modes, mode_order)
    sizes = (2, spans // 2, passages)
    amplitudes = amplitude_sum(partial_value, plane_index.shape[0], mode_order.shape[0], sizes)
    return (next_state, amplitudes)


def solution(mesh):
    return jax.shard_map(
        functools.partial(body, mesh.shape["passage"], mesh.shape["span"]),
        mesh=mesh,
        in_specs=(
            P("group", "span", "passage"),
            P(("group", "span")),
            P(("group", "span"), "passage"),
            P("group"),
            P(None, "span"),
            P(),
        ),
        out_specs=(P("group", "span", "passage"), P("group", None, None)),
        check_vma=False,
    )
```
